32 devices in a mesh: group: 2 (over y), box: 16 (over z, x, core).
Axes of the slice: x: 2, y: 2, z: 4, core: 2. Of those that a mesh axis runs over, the one named last changes fastest.
Arguments:
- dipoles: float32 [3, 8192], P(None, ('group', 'box')), may hold values from -6 to 6
- perm_field: float32 [3, 8192], P(None, ('group', 'box')), may hold values from -6 to 6
- positions: float32 [3, 8192], P(None, ('group', 'box')), may hold values from -1 to 1
- polarizability: float32 [8192], P(('group', 'box')), may hold values from 0.5 to 2.5
- occupancy: int32 [64], P(('group', 'box')), may hold values from 1 to 128
- far_boxes: int32 [64, 189], P(('group', 'box')), may hold values from 0 to 63, as said below
- far_class: int32 [64, 189], P(('group', 'box')), may hold values from 0 to 7
- far_count: int32 [64], P(('group', 'box')), may hold values from 94 to 189
- far_scale: float32 [64, 189], P(('group', 'box')), may hold values from 0.2 to 1
- translations: float32 [8, 165, 165], replicated, may hold values from -0.0015015624 to 0.0015015624
Outputs:
- new_dipoles: float32 [3, 8192], P(None, ('group', 'box'))
- residual: float32 [3, 8192], P(None, ('group', 'box'))
The draws below stay inside these ranges and needn't reach their ends.
Inputs may be any that keep to these rules, and one draw needn't show every extreme that they name: Entry far_boxes[b, e] names a box of layer z' in group g' with |z' - z| <= 4 for box b's own layer z and group g, and |z' - z| >= 2 where g' = g; the first entry of every list is 4 layers away.
All inputs are finite; a program needn't handle non-finite values.
Results may differ from the reference program's by a relative error of at most 0.0003.
Values sent between devices are 32-bit elements; how exact they have to be, the bound alone decides.
A program may use at most 64 MiB of HBM per device.

```python
import math
import jax
import jax.numpy as jnp
import numpy as np
from jax import lax

TILE = 128
ORDER = 8
NTERM = 165
FX = 2
FY = 1
BOX_DEV = 2
ILIST = 189
REACH = 4
CLASSES = 8
GROUPS = 2
OWNERS = 16
BOXES = 64
ATOMS = 8192


def draw_far_boxes(key, part):
    numbers = jnp.arange(BOXES, dtype=jnp.int32)
    layer = numbers // BOX_DEV % OWNERS
    home_group = numbers // (BOX_DEV * OWNERS)
    key_group, key_step, key_far, key_slot = jax.random.split(key, 4)
    target_group = jax.random.randint(key_group, (BOXES, ILIST), 0, GROUPS)
    stride = jax.random.randint(key_step, (BOXES, ILIST), 0, 2 * REACH + 1) - REACH
    direction = jnp.where(stride >= 0, 1, -1)
    far_step = direction * jax.random.randint(key_far, (BOXES, ILIST), 2, REACH + 1)
    too_close = (target_group == home_group[:, None]) & (jnp.abs(stride) < 2)
    stride = jnp.where(too_close, far_step, stride)
    stride = stride.at[:, 0].set(REACH)
    landing = layer[:, None] + stride
    stride = jnp.where((landing < 0) | (landing >= OWNERS), -stride, stride)
    within = jax.random.randint(key_slot, (BOXES, ILIST), 0, BOX_DEV)
    result = (target_group * OWNERS + layer[:, None] + stride) * BOX_DEV + within
    return result.astype(jnp.int32)


def with_ends(values, key, least, top_value):
    extent = values.shape
    place = [jax.random.randint(jax.random.fold_in(key, axis), (), 0, extent[axis]) for axis in range(len(extent))]
    values = values.at[tuple(place)].set(least)
    longest = extent.index(max(extent))
    place[longest] = (place[longest] + 1) % extent[longest]
    return values.at[tuple(place)].set(top_value)


def block_scale(rng, extent, shards, low, top_value):
    def one(position, shards_of):
        heights = jax.random.uniform(jax.random.fold_in(jax.random.fold_in(rng, 6), position), (shards_of,), jnp.float32, low / len(shards), top_value / len(shards))
        return jnp.repeat(jnp.exp(heights), extent[position] // shards_of).reshape((-1,) + (1,) * (len(extent) - position - 1))

    factor_of = one(*shards[0])
    for cut in shards[1:]:
        factor_of = factor_of * one(*cut)
    return factor_of


def centred(key, shape, width, reach, pieces=(), kind=jnp.bfloat16):
    entries = width * jax.random.normal(key, shape, jnp.float32)
    if pieces:
        entries = entries * block_scale(key, shape, pieces, -0.22, 0.18)
    return jnp.clip(entries, -reach, reach).astype(kind)


def setup_inputs(seed: int = 0) -> dict:
    key_list = jax.random.split(jax.random.key(seed), 11)
    return {
        "dipoles": centred(key_list[0], (3, ATOMS), 1.0, 6.0, ((1, 32),), jnp.float32),
        "perm_field": centred(key_list[1], (3, ATOMS), 1.0, 6.0, ((1, 32),), jnp.float32),
        "positions": jnp.clip(jax.random.uniform(key_list[2], (3, ATOMS), jnp.float32, -1.0, 1.0) * block_scale(key_list[2], (3, ATOMS), ((1, 32),), -0.4, 0.0), -1.0, 1.0),
        "polarizability": jnp.clip(jnp.exp(math.log(2.5) - 1.609438 * jax.random.uniform(key_list[3], (ATOMS,), jnp.float32) ** block_scale(key_list[3], (ATOMS,), ((0, 32),), -0.2, 0.2)), 0.5, 2.5),
        "occupancy": with_ends(jax.random.randint(key_list[4], (BOXES,), 1, TILE + 1), jax.random.fold_in(key_list[4], 1), 1, TILE).astype(jnp.int32),
        "far_boxes": draw_far_boxes(jax.random.fold_in(key_list[10], 71), 0),
        "far_class": with_ends(jax.random.randint(key_list[6], (BOXES, ILIST), 0, CLASSES), jax.random.fold_in(key_list[6], 1), 0, CLASSES - 1).astype(jnp.int32),
        "far_count": with_ends(jax.random.randint(key_list[7], (BOXES,), ILIST // 2, ILIST + 1), jax.random.fold_in(key_list[7], 1), ILIST // 2, ILIST).astype(jnp.int32),
        "far_scale": jnp.clip(jnp.exp(math.log(1.0) - 1.609438 * jax.random.uniform(key_list[8], (BOXES, ILIST), jnp.float32) ** block_scale(key_list[8], (BOXES, ILIST), ((0, 32),), -0.2, 0.2)), 0.2, 1.0),
        "translations": centred(key_list[9], (CLASSES, NTERM, NTERM), (0.5 * (NTERM * ILIST * TILE) ** -0.5), 0.0015015624, (), jnp.float32),
    }


HALF = 5.4
THOLE = 0.39
SOFT = 1.0
HIGH = lax.Precision.HIGHEST

def term_table(order):
    listing = []
    for degree in range(order + 1):
        for first_idx in range(degree + 1):
            for second_idx in range(degree + 1 - first_idx):
                listing.append((first_idx, second_idx, degree - first_idx - second_idx))
    return np.array(listing, dtype=np.int32)

def chebyshev(coord, order):
    series = [jnp.ones_like(coord), coord]
    for number in range(2, order + 1):
        series.append(2.0 * coord * series[-1] - series[-2])
    return jnp.stack(series[:order + 1])

def monomials(positions):
    table = term_table(ORDER)
    cheb_x = chebyshev(positions[0], ORDER)
    cheb_y = chebyshev(positions[1], ORDER)
    cheb_z = chebyshev(positions[2], ORDER)
    return cheb_x[table[:, 0]] * cheb_y[table[:, 1]] * cheb_z[table[:, 2]]

def pair_field(target_rel, target_root, source_rel, source_root, source_dip, offset, keep_mask):
    deltas = [HALF * (target_rel[component][:, :, None] - source_rel[component][:, None, :] - 2.0 * offset[component]) for component in range(3)]
    squared = deltas[0] * deltas[0] + deltas[1] * deltas[1] + deltas[2] * deltas[2] + SOFT
    inverse = lax.rsqrt(squared)
    cube_inv = inverse * inverse * inverse
    strength = THOLE * squared * jnp.sqrt(squared) * target_root[:, :, None] * source_root[:, None, :]
    damping = jnp.exp(-strength)
    lambda_three = -jnp.expm1(-strength)
    lambda_five = lambda_three - strength * damping
    projection = deltas[0] * source_dip[0][:, None, :] + deltas[1] * source_dip[1][:, None, :] + deltas[2] * source_dip[2][:, None, :]
    radial = keep_mask * 3.0 * lambda_five * cube_inv * inverse * inverse * projection
    direct = keep_mask * lambda_three * cube_inv
    return jnp.stack([lax.optimization_barrier(jnp.sum(deltas[component] * radial - direct * source_dip[component][:, None, :], axis=2)) for component in range(3)])

def near_field(source, positions, root_pol):
    shape = (GROUPS, OWNERS, FX, FY, TILE)
    padding = ((0, 0), (1, 1), (1, 1), (1, 1), (0, 0))
    src_dip = jnp.moveaxis(jnp.pad(source.reshape((3,) + shape), ((0, 0),) + padding), 1, 0)
    src_rel = jnp.moveaxis(jnp.pad(positions.reshape((3,) + shape), ((0, 0),) + padding), 1, 0)
    src_root = jnp.pad(root_pol.reshape(shape), padding)
    tgt_rel = jnp.moveaxis(positions.reshape((3,) + shape), 1, 0)
    tgt_root = root_pol.reshape(shape)
    boxes = OWNERS * FX * FY

    def per_group(inputs):
        dip_g, rel_g, root_g, trel_g, troot_g = inputs
        target_rel = trel_g.reshape(3, boxes, TILE)
        target_root = troot_g.reshape(boxes, TILE)
        total = jnp.zeros((3, boxes, TILE), jnp.float32)
        for shift_z in (-1, 0, 1):
            for shift_x in (-1, 0, 1):
                for shift_y in (-1, 0, 1):
                    window_dip = dip_g[:, 1 + shift_z:1 + shift_z + OWNERS, 1 + shift_x:1 + shift_x + FX, 1 + shift_y:1 + shift_y + FY].reshape(3, boxes, TILE)
                    window_rel = rel_g[:, 1 + shift_z:1 + shift_z + OWNERS, 1 + shift_x:1 + shift_x + FX, 1 + shift_y:1 + shift_y + FY].reshape(3, boxes, TILE)
                    window_root = root_g[1 + shift_z:1 + shift_z + OWNERS, 1 + shift_x:1 + shift_x + FX, 1 + shift_y:1 + shift_y + FY].reshape(boxes, TILE)
                    if shift_z == 0 and shift_x == 0 and (shift_y == 0):
                        keep_mask = 1.0 - jnp.eye(TILE, dtype=jnp.float32)
                    else:
                        keep_mask = jnp.float32(1.0)
                    total = total + pair_field(target_rel, target_root, window_rel, window_root, window_dip, (float(shift_x), float(shift_y), float(shift_z)), keep_mask)
        return total
    fields = lax.map(per_group, (src_dip, src_rel, src_root, tgt_rel, tgt_root))
    return jnp.moveaxis(fields, 1, 0).reshape(3, -1)

def far_field(source, monomial, far_boxes, far_class, far_count, far_scale, translations):
    mono_b = monomial.reshape(NTERM, BOXES, TILE)
    dip_b = source.reshape(3, BOXES, TILE)
    multipole = jnp.einsum('tbs,cbs->bct', mono_b, dip_b, precision=HIGH).reshape(BOXES, 3 * NTERM)
    listing = lax.broadcasted_iota(jnp.int32, (BOXES, ILIST), 1)
    weights = far_scale * (listing < far_count[:, None]).astype(jnp.float32)
    classes = (far_class[:, :, None] == lax.broadcasted_iota(jnp.int32, (1, 1, CLASSES), 2)).astype(jnp.float32) * weights[:, :, None]
    blocks = BOXES // BOX_DEV

    def per_block(inputs):
        box_ids, class_w = inputs
        picked = multipole[box_ids.astype(jnp.int32)]
        return jnp.einsum('bjo,bjq->boq', class_w, picked, precision=HIGH)
    summed = lax.map(per_block, (far_boxes.reshape(blocks, BOX_DEV, ILIST), classes.reshape(blocks, BOX_DEV, ILIST, CLASSES)))
    summed = summed.reshape(BOXES, CLASSES, 3, NTERM)
    local = jnp.einsum('bocu,otu->bct', summed, translations, precision=HIGH)
    return jnp.einsum('tbs,bct->cbs', mono_b, local, precision=HIGH).reshape(3, ATOMS)

def reference(dipoles, perm_field, positions, polarizability, occupancy, far_boxes, far_class, far_count, far_scale, translations):
    slot = lax.broadcasted_iota(jnp.int32, (BOXES, TILE), 1)
    live_mask = (slot < occupancy[:, None]).astype(jnp.float32).reshape(-1)
    source = dipoles * live_mask
    root_pol = lax.rsqrt(polarizability)
    monomial = monomials(positions)
    far_part = far_field(source, monomial, far_boxes, far_class, far_count, far_scale, translations)
    near_zero = near_field(source, positions, root_pol)
    residual = live_mask * (perm_field + far_part + near_zero - source / polarizability)
    sweep_one = polarizability * residual
    sweep_two = live_mask * polarizability * (residual + near_field(sweep_one, positions, root_pol))
    sweep_three = live_mask * polarizability * (residual + near_field(sweep_two, positions, root_pol))
    return (source + sweep_three, residual)
```

```python
import functools
import jax
import jax.numpy as jnp
import numpy as np
from jax import lax
from jax.experimental import pallas as pl
from jax.experimental.pallas import tpu as pltpu
from jax.sharding import PartitionSpec as P

TILE = 128
ORDER = 8
FX = 2
FY = 1
REACH = 4
SPAN = 2 * REACH + 1
WIDE = 256
ROWS = 16

HALF = 5.4
THOLE = 0.39
SOFT = 1.0
MESH = pl.DeviceIdType.MESH
F32 = jnp.float32
BF16 = jnp.bfloat16
LANES = (((1,), (1,)), ((), ()))
PLAIN = (((1,), (0,)), ((), ()))


def term_table(order):
    listing = []
    for degree in range(order + 1):
        for first_idx in range(degree + 1):
            for second_idx in range(degree + 1 - first_idx):
                listing.append((first_idx, second_idx, degree - first_idx - second_idx))
    return np.array(listing, dtype=np.int32)


def pick_matrix():
    table = term_table(ORDER)
    pick = np.zeros((3, WIDE, 64), np.float32)
    for term, powers in enumerate(table):
        for axis in range(3):
            for part in range(2):
                pick[axis, term, 32 * part + 3 * powers[axis] + axis] = 1.0
    return pick.reshape(3 * WIDE, 64)


def split(x):
    high = x.astype(BF16)
    return high, (x - high.astype(F32)).astype(BF16)


def dot(a, b, dims):
    return lax.dot_general(a, b, dims, preferred_element_type=F32)


def dot_parts(a, b, dims):
    return dot(a[0], b[0], dims) + (dot(a[0], b[1], dims) + dot(a[1], b[0], dims))


def kernel(
    groups, owners,
    dip_ref, perm_ref, pos_ref, pol_ref, occ_ref, fbox_ref, fcls_ref, fcnt_ref, fscl_ref,
    trans_ref, pick_ref,
    new_ref, res_ref,
    own, beside, geo_t, mono_ref, window, tensor, acc,
    nsend, nrecv, wsend, wrecv,
):
    group = lax.axis_index("group")
    layer = lax.axis_index("box")

    def in_range(step):
        place = layer + step
        return jnp.logical_and(place >= 0, place < owners)

    def neighbour(step):
        return jnp.clip(layer + step, 0, owners - 1)

    def far_peers(act):
        for peer_group in range(groups):
            for step in range(-REACH, REACH + 1):
                ok = in_range(step) if step else group != peer_group
                pl.when(ok)(functools.partial(act, peer_group, step))

    barrier = pltpu.get_barrier_semaphore()

    def greet(peer_group, step):
        pl.semaphore_signal(
            barrier, inc=1, device_id=(peer_group, neighbour(step)), device_id_type=MESH
        )

    far_peers(greet)

    for step in range(-REACH, REACH + 1):
        if step:

            @pl.when(jnp.logical_not(in_range(step)))
            def _(step=step):
                for peer_group in range(groups):
                    window[peer_group * SPAN + step + REACH] = jnp.zeros((8, WIDE), F32)

    for side, step in enumerate((-1, 1)):

        @pl.when(jnp.logical_not(in_range(step)))
        def _(side=side):
            for turn in range(3):
                beside[turn, side] = jnp.zeros((8, WIDE), F32)

    lane = lax.broadcasted_iota(jnp.int32, (1, 2 * TILE), 1)
    second = lane >= TILE
    slot = jnp.where(second, lane - TILE, lane)
    live = (slot < jnp.where(second, occ_ref[1:2], occ_ref[0:1])).astype(F32)
    pol = pol_ref[...]
    root = lax.rsqrt(pol)
    pos = pos_ref[...]
    source = dip_ref[...] * live
    place_x = HALF * (pos[0:1] + jnp.where(second, 2.0, 0.0))
    own[0] = jnp.concatenate(
        [place_x, HALF * pos[1:3], root, source, jnp.zeros((1, WIDE), F32)], axis=0
    )
    geo_t[...] = jnp.transpose(own[0])

    series = [jnp.ones_like(pos), pos]
    for _ in range(2, ORDER + 1):
        series.append(2.0 * pos * series[-1] - series[-2])
    cheb = jnp.concatenate(series + [jnp.zeros((5, WIDE), F32)], axis=0)
    planes = dot(pick_ref[...], jnp.concatenate(split(cheb), axis=0), PLAIN)
    mono = planes[0:WIDE] * planes[WIDE : 2 * WIDE] * planes[2 * WIDE :]
    mono_ref[...] = mono
    first_half = jnp.where(second, 0.0, source)
    second_half = source - first_half
    moments = jnp.concatenate([first_half, second_half, jnp.zeros((2, WIDE), F32)], axis=0)
    window[group * SPAN + REACH] = dot_parts(split(moments), split(mono), LANES)

    below = jnp.minimum(layer, REACH)
    above = jnp.minimum(owners - 1 - layer, REACH)
    pl.semaphore_wait(barrier, (below + above + 1) * groups - 1)

    def near_copy(turn, side, step):
        return pltpu.make_async_remote_copy(
            src_ref=own.at[turn],
            dst_ref=beside.at[turn, side],
            send_sem=nsend.at[2 * turn + side],
            recv_sem=nrecv.at[2 * turn + side],
            device_id=(group, neighbour(step)),
            device_id_type=MESH,
        )

    def near_send(turn):
        for side, step in enumerate((1, -1)):
            pl.when(in_range(step))(
                lambda side=side, step=step: near_copy(turn, side, step).start()
            )

    def near_wait(turn):
        for side, step in enumerate((-1, 1)):
            pl.when(in_range(step))(
                lambda side=side, step=step: near_copy(turn, side, step).wait_recv()
            )

    near_send(0)

    def far_send(peer_group, step):
        pltpu.make_async_remote_copy(
            src_ref=window.at[group * SPAN + REACH],
            dst_ref=window.at[group * SPAN + REACH - step],
            send_sem=wsend.at[peer_group * SPAN + REACH + step],
            recv_sem=wrecv.at[group * SPAN + REACH - step],
            device_id=(peer_group, neighbour(step)),
            device_id_type=MESH,
        ).start()

    far_peers(far_send)

    def far_copy(peer_group, step):
        place = peer_group * SPAN + REACH + step
        return pltpu.make_async_remote_copy(
            src_ref=window.at[group * SPAN + REACH],
            dst_ref=window.at[place],
            send_sem=wsend.at[place],
            recv_sem=wrecv.at[place],
            device_id=(peer_group, neighbour(step)),
            device_id_type=MESH,
        )

    def build(number, load, shift):
        def body(block, carry):
            rows = pl.ds(pl.multiple_of(block * ROWS, ROWS), ROWS)
            target = geo_t[rows, :]
            total = [None] * 3
            for half in range(2):
                geo = load(half)
                delta = [target[:, axis : axis + 1] - geo[axis : axis + 1] for axis in range(2)]
                delta.append(target[:, 2:3] - (geo[2:3] + 2.0 * HALF * shift))
                squared = delta[0] * delta[0] + delta[1] * delta[1] + (delta[2] * delta[2] + SOFT)
                inverse = lax.rsqrt(squared)
                strength = squared * squared * inverse * (THOLE * target[:, 3:4] * geo[3:4])
                damping = jnp.exp(-strength)
                lambda_three = 1.0 - damping
                lambda_five = lambda_three - strength * damping
                inverse_two = inverse * inverse
                cube = inverse_two * inverse
                direct = lambda_three * cube
                radial = 3.0 * lambda_five * (cube * inverse_two)
                if number == 0:
                    shape = (ROWS, TILE)
                    here = block * ROWS + lax.broadcasted_iota(jnp.int32, shape, 0)
                    other = half * TILE + lax.broadcasted_iota(jnp.int32, shape, 1)
                    keep = here != other
                    direct = jnp.where(keep, direct, 0.0)
                    radial = jnp.where(keep, radial, 0.0)
                scaled = [radial * part for part in delta]
                entries = [
                    scaled[0] * delta[0] - direct,
                    scaled[1] * delta[1] - direct,
                    scaled[2] * delta[2] - direct,
                    scaled[0] * delta[1],
                    scaled[0] * delta[2],
                    scaled[1] * delta[2],
                ]
                for index, entry in enumerate(entries):
                    tensor[2 * number + half, index, rows, :] = entry
                total = gather(total, entries, [geo[4:5], geo[5:6], geo[6:7]])
            for axis in range(3):
                if number == 0:
                    acc[axis, rows, :] = total[axis]
                else:
                    acc[axis, rows, :] += total[axis]
            return carry

        lax.fori_loop(0, 2 * TILE // ROWS, body, 0)

    def gather(total, m, q):
        terms = [
            m[0] * q[0] + m[3] * q[1] + m[4] * q[2],
            m[3] * q[0] + m[1] * q[1] + m[5] * q[2],
            m[4] * q[0] + m[5] * q[1] + m[2] * q[2],
        ]
        return [t if old is None else old + t for old, t in zip(total, terms)]

    def apply(numbers, rows_of, first):
        parts = [
            [rows_of(number)[axis : axis + 1, half * TILE : (half + 1) * TILE] for axis in range(3)]
            for number in numbers
            for half in range(2)
        ]

        def body(block, carry):
            rows = pl.ds(pl.multiple_of(block * ROWS, ROWS), ROWS)
            total = [None] * 3 if first else [acc[axis, rows, :] for axis in range(3)]
            for place, number in enumerate(numbers):
                for half in range(2):
                    entries = [tensor[2 * number + half, index, rows, :] for index in range(6)]
                    total = gather(total, entries, parts[2 * place + half])
            for axis in range(3):
                acc[axis, rows, :] = total[axis]
            return carry

        lax.fori_loop(0, 2 * TILE // ROWS, body, 0)

    def collect():
        row = lax.broadcasted_iota(jnp.int32, (8, 2 * TILE), 0)
        total = None
        for axis in range(3):
            unit = (row == axis).astype(F32).astype(BF16)
            part = dot(unit, jnp.concatenate(split(acc[axis]), axis=1), LANES)
            total = part if total is None else total + part
        return total[0:3]

    build(0, lambda half: own[0, :, half * TILE : (half + 1) * TILE], 0.0)

    ilist = fbox_ref.shape[1]
    flat_rows = window.shape[0] * 8
    row = lax.broadcasted_iota(jnp.int32, (flat_rows, 1), 0)
    place, inner = row >> 3, row & 7
    owner_group = jnp.zeros_like(place)
    for peer_group in range(1, groups):
        owner_group += (place >= peer_group * SPAN).astype(jnp.int32)
    number = (owner_group * (owners - SPAN) + place + (layer - REACH)) * (FX * FY)
    number = number + (inner >= 3).astype(jnp.int32)
    number = jnp.where(inner < 6, number, -1)
    line = lax.broadcasted_iota(jnp.int32, (64, ilist), 0)
    entry = lax.broadcasted_iota(jnp.int32, (64, ilist), 1)
    selector = None
    for box in range(FX * FY):
        match = (fbox_ref[box : box + 1] == number).astype(F32).astype(BF16)
        inside = line & 7
        mine = jnp.logical_and(inside >= 3 * box, inside < 3 * box + 3)
        mine = jnp.logical_and(mine, entry < fcnt_ref[box : box + 1])
        mine = jnp.logical_and(mine, fcls_ref[box : box + 1] == (line >> 3))
        weights = split(jnp.where(mine, fscl_ref[box : box + 1], 0.0))
        part = dot(weights[0], match, LANES) + dot(weights[1], match, LANES)
        selector = part if selector is None else selector + part
    left = lax.broadcasted_iota(jnp.int32, selector.shape, 0) & 7
    right = lax.broadcasted_iota(jnp.int32, selector.shape, 1) & 7
    left = jnp.where(left >= 3, left - 3, left)
    right = jnp.where(right >= 3, right - 3, right)
    selector = split(jnp.where(left == right, selector, 0.0))

    near_wait(0)
    for side, shift in enumerate((-1.0, 1.0)):
        build(
            side + 1,
            lambda half, side=side: beside[0, side, :, half * TILE : (half + 1) * TILE],
            shift,
        )
    near_zero = collect()

    far_peers(lambda peer_group, step: far_copy(peer_group, step).wait_recv())
    summed = dot_parts(selector, split(window[...].reshape(flat_rows, WIDE)), PLAIN)
    nterm = trans_ref.shape[1]
    local = None
    for index in range(trans_ref.shape[0]):
        part = dot_parts(
            split(summed[8 * index : 8 * index + 8, 0:nterm]), split(trans_ref[index]), LANES
        )
        local = part if local is None else local + part
    spread = dot_parts(split(local), split(mono_ref[0:nterm]), PLAIN)
    far_part = jnp.where(second, spread[3:6], spread[0:3])

    residual = live * (perm_ref[...] + far_part + near_zero - source / pol)
    res_ref[...] = residual
    sweep = pol * residual
    for turn in (1, 2):
        own[turn] = jnp.concatenate([sweep, jnp.zeros((5, WIDE), F32)], axis=0)
        near_send(turn)
        apply((0,), lambda _, turn=turn: own[turn], True)
        near_wait(turn)
        apply((1, 2), lambda number, turn=turn: beside[turn, number - 1], False)
        sweep = live * pol * (residual + collect())
    new_ref[...] = source + sweep

    for turn in range(3):
        for side, step in enumerate((1, -1)):
            pl.when(in_range(step))(
                lambda turn=turn, side=side, step=step: near_copy(turn, side, step).wait_send()
            )
    far_peers(lambda peer_group, step: far_copy(peer_group, step).wait_send())


def solution(mesh):
    groups, owners = mesh.shape["group"], mesh.shape["box"]

    def on_device(dip, perm, pos, pol, occ, fbox, fcls, fcnt, fscl, trans):
        vmem = pl.BlockSpec(memory_space=pltpu.VMEM)
        slots = groups * SPAN
        return pl.pallas_call(
            functools.partial(kernel, groups, owners),
            out_shape=(jax.ShapeDtypeStruct(dip.shape, F32),) * 2,
            in_specs=[vmem] * 11,
            out_specs=(vmem, vmem),
            scratch_shapes=[
                pltpu.VMEM((3, 8, WIDE), F32),
                pltpu.VMEM((3, 2, 8, WIDE), F32),
                pltpu.VMEM((WIDE, 8), F32),
                pltpu.VMEM((WIDE, WIDE), F32),
                pltpu.VMEM((slots, 8, WIDE), F32),
                pltpu.VMEM((6, 6, 2 * TILE, TILE), F32),
                pltpu.VMEM((3, 2 * TILE, TILE), F32),
                pltpu.SemaphoreType.DMA((6,)),
                pltpu.SemaphoreType.DMA((6,)),
                pltpu.SemaphoreType.DMA((slots,)),
                pltpu.SemaphoreType.DMA((slots,)),
            ],
            compiler_params=pltpu.CompilerParams(
                collective_id=0, has_side_effects=True, vmem_limit_bytes=40 * 1024 * 1024
            ),
        )(
            dip, perm, pos, pol.reshape(1, -1), occ.reshape(-1, 1), fbox, fcls, fcnt.reshape(-1, 1),
            fscl, trans,
            jnp.asarray(pick_matrix(), BF16),
        )

    split_dim = ("group", "box")
    return jax.shard_map(
        on_device,
        mesh=mesh,
        in_specs=(
            P(None, split_dim), P(None, split_dim), P(None, split_dim), P(split_dim),
            P(split_dim), P(split_dim, None), P(split_dim, None), P(split_dim),
            P(split_dim, None), P(),
        ),
        out_specs=(P(None, split_dim), P(None, split_dim)),
        check_vma=False,
    )
```

```python
import functools
import jax
import jax.numpy as jnp
import numpy as np
from jax import lax
from jax.experimental import pallas as pl
from jax.experimental.pallas import tpu as pltpu
from jax.sharding import PartitionSpec as P

TILE = 128
ORDER = 8
FX = 2
FY = 1
REACH = 4
SPAN = 2 * REACH + 1
WIDE = 256
ROWS = 16

HALF = 5.4
THOLE = 0.39
SOFT = 1.0
MESH = pl.DeviceIdType.MESH
F32 = jnp.float32
BF16 = jnp.bfloat16
LANES = (((1,), (1,)), ((), ()))
PLAIN = (((1,), (0,)), ((), ()))


def term_table(order):
    listing = []
    for degree in range(order + 1):
        for first_idx in range(degree + 1):
            for second_idx in range(degree + 1 - first_idx):
                listing.append((first_idx, second_idx, degree - first_idx - second_idx))
    return np.array(listing, dtype=np.int32)


def pick_matrix():
    table = term_table(ORDER)
    pick = np.zeros((3, WIDE, 64), np.float32)
    for term, powers in enumerate(table):
        for axis in range(3):
            for part in range(2):
                pick[axis, term, 32 * part + 3 * powers[axis] + axis] = 1.0
    return pick.reshape(3 * WIDE, 64)


def split(x):
    high = x.astype(BF16)
    return high, (x - high.astype(F32)).astype(BF16)


def dot(a, b, dims):
    return lax.dot_general(a, b, dims, preferred_element_type=F32)


def dot_parts(a, b, dims):
    return dot(a[0], b[0], dims) + (dot(a[0], b[1], dims) + dot(a[1], b[0], dims))


def kernel(
    groups, owners,
    dip_ref, perm_ref, pos_ref, pol_ref, occ_ref, fbox_ref, fcls_ref, fcnt_ref, fscl_ref,
    trans_ref, pick_ref,
    new_ref, res_ref,
    own, beside, geo_t, mono_ref, window, tensor, acc,
    nsend, nrecv, wsend, wrecv,
):
    group = lax.axis_index("group")
    layer = lax.axis_index("box")

    def in_range(step):
        place = layer + step
        return jnp.logical_and(place >= 0, place < owners)

    def neighbour(step):
        return jnp.clip(layer + step, 0, owners - 1)

    def far_peers(act):
        for peer_group in range(groups):
            for step in range(-REACH, REACH + 1):
                ok = in_range(step) if step else group != peer_group
                pl.when(ok)(functools.partial(act, peer_group, step))

    barrier = pltpu.get_barrier_semaphore()

    def greet(peer_group, step):
        pl.semaphore_signal(
            barrier, inc=1, device_id=(peer_group, neighbour(step)), device_id_type=MESH
        )

    far_peers(greet)

    for step in range(-REACH, REACH + 1):
        if step:

            @pl.when(jnp.logical_not(in_range(step)))
            def _(step=step):
                for peer_group in range(groups):
                    window[peer_group * SPAN + step + REACH] = jnp.zeros((8, WIDE), F32)

    for side, step in enumerate((-1, 1)):

        @pl.when(jnp.logical_not(in_range(step)))
        def _(side=side):
            for turn in range(3):
                beside[turn, side] = jnp.zeros((8, WIDE), F32)

    lane = lax.broadcasted_iota(jnp.int32, (1, 2 * TILE), 1)
    second = lane >= TILE
    slot = jnp.where(second, lane - TILE, lane)
    occ = occ_ref[...]
    live = (slot < jnp.where(second, occ[:, 1:2], occ[:, 0:1])).astype(F32)
    pol = pol_ref[...]
    root = lax.rsqrt(pol)
    pos = pos_ref[...]
    source = dip_ref[...] * live
    place_x = HALF * (pos[0:1] + jnp.where(second, 2.0, 0.0))
    own[0] = jnp.concatenate(
        [place_x, HALF * pos[1:3], root, source, jnp.zeros((1, WIDE), F32)], axis=0
    )
    geo_t[...] = jnp.transpose(own[0])

    series = [jnp.ones_like(pos), pos]
    for _ in range(2, ORDER + 1):
        series.append(2.0 * pos * series[-1] - series[-2])
    cheb = jnp.concatenate(series + [jnp.zeros((5, WIDE), F32)], axis=0)
    planes = dot(pick_ref[...], jnp.concatenate(split(cheb), axis=0), PLAIN)
    mono = planes[0:WIDE] * planes[WIDE : 2 * WIDE] * planes[2 * WIDE :]
    mono_ref[...] = mono
    first_half = jnp.where(second, 0.0, source)
    second_half = source - first_half
    moments = jnp.concatenate([first_half, second_half, jnp.zeros((2, WIDE), F32)], axis=0)
    window[group * SPAN + REACH] = dot_parts(split(moments), split(mono), LANES)

    below = jnp.minimum(layer, REACH)
    above = jnp.minimum(owners - 1 - layer, REACH)
    pl.semaphore_wait(barrier, (below + above + 1) * groups - 1)

    def near_copy(turn, side, step):
        return pltpu.make_async_remote_copy(
            src_ref=own.at[turn],
            dst_ref=beside.at[turn, side],
            send_sem=nsend.at[2 * turn + side],
            recv_sem=nrecv.at[2 * turn + side],
            device_id=(group, neighbour(step)),
            device_id_type=MESH,
        )

    def near_send(turn):
        for side, step in enumerate((1, -1)):
            pl.when(in_range(step))(
                lambda side=side, step=step: near_copy(turn, side, step).start()
            )

    def near_wait(turn):
        for side, step in enumerate((-1, 1)):
            pl.when(in_range(step))(
                lambda side=side, step=step: near_copy(turn, side, step).wait_recv()
            )

    near_send(0)

    def far_send(peer_group, step):
        pltpu.make_async_remote_copy(
            src_ref=window.at[group * SPAN + REACH],
            dst_ref=window.at[group * SPAN + REACH - step],
            send_sem=wsend.at[peer_group * SPAN + REACH + step],
            recv_sem=wrecv.at[group * SPAN + REACH - step],
            device_id=(peer_group, neighbour(step)),
            device_id_type=MESH,
        ).start()

    far_peers(far_send)

    def far_copy(peer_group, step):
        place = peer_group * SPAN + REACH + step
        return pltpu.make_async_remote_copy(
            src_ref=window.at[group * SPAN + REACH],
            dst_ref=window.at[place],
            send_sem=wsend.at[place],
            recv_sem=wrecv.at[place],
            device_id=(peer_group, neighbour(step)),
            device_id_type=MESH,
        )

    def build(layers, size):
        def body(block, carry):
            rows = pl.ds(pl.multiple_of(block * size, size), size)
            target = geo_t[rows, :]
            total = [None] * 3
            for number, load, shift, half in [one + (h,) for one in layers for h in range(2)]:
                geo = load(half)
                delta = [target[:, axis : axis + 1] - geo[axis : axis + 1] for axis in range(2)]
                delta.append(target[:, 2:3] - (geo[2:3] + 2.0 * HALF * shift))
                squared = delta[0] * delta[0] + delta[1] * delta[1] + (delta[2] * delta[2] + SOFT)
                inverse = lax.rsqrt(squared)
                strength = squared * squared * inverse * (THOLE * target[:, 3:4] * geo[3:4])
                damping = jnp.exp(-strength)
                lambda_three = 1.0 - damping
                lambda_five = lambda_three - strength * damping
                inverse_two = inverse * inverse
                cube = inverse_two * inverse
                direct = lambda_three * cube
                radial = 3.0 * lambda_five * (cube * inverse_two)
                if number == 0:
                    shape = (size, TILE)
                    here = block * size + lax.broadcasted_iota(jnp.int32, shape, 0)
                    other = half * TILE + lax.broadcasted_iota(jnp.int32, shape, 1)
                    keep = here != other
                    direct = jnp.where(keep, direct, 0.0)
                    radial = jnp.where(keep, radial, 0.0)
                scaled = [radial * part for part in delta]
                entries = [
                    scaled[0] * delta[0] - direct,
                    scaled[1] * delta[1] - direct,
                    scaled[2] * delta[2] - direct,
                    scaled[0] * delta[1],
                    scaled[0] * delta[2],
                    scaled[1] * delta[2],
                ]
                for index, entry in enumerate(entries):
                    tensor[2 * number + half, index, rows, :] = entry
                total = gather(total, entries, [geo[4:5], geo[5:6], geo[6:7]])
            for axis in range(3):
                if layers[0][0] == 0:
                    acc[axis, rows, :] = total[axis]
                else:
                    acc[axis, rows, :] += total[axis]
            return carry

        lax.fori_loop(0, 2 * TILE // size, body, 0)

    def gather(total, m, q):
        terms = [
            m[0] * q[0] + m[3] * q[1] + m[4] * q[2],
            m[3] * q[0] + m[1] * q[1] + m[5] * q[2],
            m[4] * q[0] + m[5] * q[1] + m[2] * q[2],
        ]
        return [t if old is None else old + t for old, t in zip(total, terms)]

    def apply(numbers, rows_of, first):
        parts = [
            [rows_of(number)[axis : axis + 1, half * TILE : (half + 1) * TILE] for axis in range(3)]
            for number in numbers
            for half in range(2)
        ]

        def body(block, carry):
            rows = pl.ds(pl.multiple_of(block * ROWS, ROWS), ROWS)
            total = [None] * 3 if first else [acc[axis, rows, :] for axis in range(3)]
            for place, number in enumerate(numbers):
                for half in range(2):
                    entries = [tensor[2 * number + half, index, rows, :] for index in range(6)]
                    total = gather(total, entries, parts[2 * place + half])
            for axis in range(3):
                acc[axis, rows, :] = total[axis]
            return carry

        lax.fori_loop(0, 2 * TILE // ROWS, body, 0)

    def collect():
        row = lax.broadcasted_iota(jnp.int32, (8, 2 * TILE), 0)
        total = None
        for axis in range(3):
            unit = (row == axis).astype(F32).astype(BF16)
            part = dot(unit, jnp.concatenate(split(acc[axis]), axis=1), LANES)
            total = part if total is None else total + part
        return total[0:3]

    build([(0, lambda half: own[0, :, half * TILE : (half + 1) * TILE], 0.0)], 32)

    ilist = fbox_ref.shape[1]
    flat_rows = window.shape[0] * 8
    row = lax.broadcasted_iota(jnp.int32, (flat_rows, 1), 0)
    place, inner = row >> 3, row & 7
    owner_group = jnp.zeros_like(place)
    for peer_group in range(1, groups):
        owner_group += (place >= peer_group * SPAN).astype(jnp.int32)
    number = (owner_group * (owners - SPAN) + place + (layer - REACH)) * (FX * FY)
    number = number + (inner >= 3).astype(jnp.int32)
    number = jnp.where(inner < 6, number, -1)
    line = lax.broadcasted_iota(jnp.int32, (64, ilist), 0)
    entry = lax.broadcasted_iota(jnp.int32, (64, ilist), 1)
    selector = None
    for box in range(FX * FY):
        match = (fbox_ref[box : box + 1] == number).astype(F32).astype(BF16)
        inside = line & 7
        mine = jnp.logical_and(inside >= 3 * box, inside < 3 * box + 3)
        mine = jnp.logical_and(mine, entry < fcnt_ref[...][:, box : box + 1])
        mine = jnp.logical_and(mine, fcls_ref[box : box + 1] == (line >> 3))
        weights = split(jnp.where(mine, fscl_ref[box : box + 1], 0.0))
        part = dot(weights[0], match, LANES) + dot(weights[1], match, LANES)
        selector = part if selector is None else selector + part
    left = lax.broadcasted_iota(jnp.int32, selector.shape, 0) & 7
    right = lax.broadcasted_iota(jnp.int32, selector.shape, 1) & 7
    left = jnp.where(left >= 3, left - 3, left)
    right = jnp.where(right >= 3, right - 3, right)
    selector = split(jnp.where(left == right, selector, 0.0))

    near_wait(0)
    build(
        [
            (side + 1, lambda half, side=side: beside[0, side, :, half * TILE : (half + 1) * TILE], shift)
            for side, shift in enumerate((-1.0, 1.0))
        ],
        16,
    )
    near_zero = collect()

    nterm, classes = trans_ref.shape[:2]
    shifted = split(trans_ref[...].reshape(nterm * classes, nterm))
    fold_shape = (nterm * classes, nterm)
    fold = lax.broadcasted_iota(jnp.int32, fold_shape, 0) >> 3
    fold = (fold == lax.broadcasted_iota(jnp.int32, fold_shape, 1)).astype(F32).astype(BF16)
    far_peers(lambda peer_group, step: far_copy(peer_group, step).wait_recv())
    summed = dot_parts(selector, split(window[...].reshape(flat_rows, WIDE)), PLAIN)
    moved = dot_parts(split(summed[:, 0:nterm]), shifted, LANES)
    wanted = lax.broadcasted_iota(jnp.int32, (8, nterm * classes), 1) & 7
    merged = None
    for index in range(classes):
        part = jnp.where(wanted == index, moved[8 * index : 8 * index + 8], 0.0)
        merged = part if merged is None else merged + part
    merged = split(merged)
    local = dot(merged[0], fold, PLAIN) + dot(merged[1], fold, PLAIN)
    spread = dot_parts(split(local), split(mono_ref[0:nterm]), PLAIN)
    far_part = jnp.where(second, spread[3:6], spread[0:3])

    residual = live * (perm_ref[...] + far_part + near_zero - source / pol)
    res_ref[...] = residual
    sweep = pol * residual
    for turn in (1, 2):
        own[turn] = jnp.concatenate([sweep, jnp.zeros((5, WIDE), F32)], axis=0)
        near_send(turn)
        apply((0,), lambda _, turn=turn: own[turn], True)
        near_wait(turn)
        apply((1, 2), lambda number, turn=turn: beside[turn, number - 1], False)
        sweep = live * pol * (residual + collect())
    new_ref[...] = source + sweep

    for turn in range(3):
        for side, step in enumerate((1, -1)):
            pl.when(in_range(step))(
                lambda turn=turn, side=side, step=step: near_copy(turn, side, step).wait_send()
            )
    far_peers(lambda peer_group, step: far_copy(peer_group, step).wait_send())


def solution(mesh):
    groups, owners = mesh.shape["group"], mesh.shape["box"]

    def on_device(dip, perm, pos, pol, occ, fbox, fcls, fcnt, fscl, trans):
        vmem = pl.BlockSpec(memory_space=pltpu.VMEM)
        slots = groups * SPAN
        return pl.pallas_call(
            functools.partial(kernel, groups, owners),
            out_shape=(jax.ShapeDtypeStruct(dip.shape, F32),) * 2,
            in_specs=[vmem] * 11,
            out_specs=(vmem, vmem),
            scratch_shapes=[
                pltpu.VMEM((3, 8, WIDE), F32),
                pltpu.VMEM((3, 2, 8, WIDE), F32),
                pltpu.VMEM((WIDE, 8), F32),
                pltpu.VMEM((WIDE, WIDE), F32),
                pltpu.VMEM((slots, 8, WIDE), F32),
                pltpu.VMEM((6, 6, 2 * TILE, TILE), F32),
                pltpu.VMEM((3, 2 * TILE, TILE), F32),
                pltpu.SemaphoreType.DMA((6,)),
                pltpu.SemaphoreType.DMA((6,)),
                pltpu.SemaphoreType.DMA((slots,)),
                pltpu.SemaphoreType.DMA((slots,)),
            ],
            compiler_params=pltpu.CompilerParams(
                collective_id=0, has_side_effects=True, vmem_limit_bytes=40 * 1024 * 1024
            ),
        )(
            dip, perm, pos, pol.reshape(1, -1), occ.reshape(1, -1), fbox, fcls, fcnt.reshape(1, -1),
            fscl, jnp.transpose(trans, (1, 0, 2)),
            jnp.asarray(pick_matrix(), BF16),
        )

    split_dim = ("group", "box")
    return jax.shard_map(
        on_device,
        mesh=mesh,
        in_specs=(
            P(None, split_dim), P(None, split_dim), P(None, split_dim), P(split_dim),
            P(split_dim), P(split_dim, None), P(split_dim, None), P(split_dim),
            P(split_dim, None), P(),
        ),
        out_specs=(P(None, split_dim), P(None, split_dim)),
        check_vma=False,
    )
```

```python
import functools
import jax
import jax.numpy as jnp
import numpy as np
from jax import lax
from jax.experimental import pallas as pl
from jax.experimental.pallas import tpu as pltpu
from jax.sharding import PartitionSpec as P

TILE = 128
ORDER = 8
FX = 2
FY = 1
REACH = 4
SPAN = 2 * REACH + 1
WIDE = 256
ROWS = 16

HALF = 5.4
THOLE = 0.39
SOFT = 1.0
MESH = pl.DeviceIdType.MESH
F32 = jnp.float32
BF16 = jnp.bfloat16
LANES = (((1,), (1,)), ((), ()))
PLAIN = (((1,), (0,)), ((), ()))


def term_table(order):
    listing = []
    for degree in range(order + 1):
        for first_idx in range(degree + 1):
            for second_idx in range(degree + 1 - first_idx):
                listing.append((first_idx, second_idx, degree - first_idx - second_idx))
    return np.array(listing, dtype=np.int32)


def pick_matrix():
    table = term_table(ORDER)
    pick = np.zeros((3, WIDE, 64), np.float32)
    for term, powers in enumerate(table):
        for axis in range(3):
            for part in range(2):
                pick[axis, term, 32 * part + 3 * powers[axis] + axis] = 1.0
    return pick.reshape(3 * WIDE, 64)


def split(x):
    high = x.astype(BF16)
    return high, (x - high.astype(F32)).astype(BF16)


def dot(a, b, dims):
    return lax.dot_general(a, b, dims, preferred_element_type=F32)


def dot_parts(a, b, dims):
    return dot(a[0], b[0], dims) + (dot(a[0], b[1], dims) + dot(a[1], b[0], dims))


def kernel(
    groups, owners,
    dip_ref, perm_ref, pos_ref, pol_ref, occ_ref, fbox_ref, fcls_ref, fcnt_ref, fscl_ref,
    trans_ref, pick_ref,
    new_ref, res_ref,
    own, beside, geo_t, mono_ref, window, tensor, acc,
    nsend, nrecv, wsend, wrecv, fetches,
):
    group = lax.axis_index("group")
    layer = lax.axis_index("box")

    def in_range(step):
        place = layer + step
        return jnp.logical_and(place >= 0, place < owners)

    def neighbour(step):
        return jnp.clip(layer + step, 0, owners - 1)

    def far_peers(act):
        for peer_group in range(groups):
            for step in range(-REACH, REACH + 1):
                ok = in_range(step) if step else group != peer_group
                pl.when(ok)(functools.partial(act, peer_group, step))

    barrier = pltpu.get_barrier_semaphore()

    def greet(peer_group, step):
        pl.semaphore_signal(
            barrier, inc=1, device_id=(peer_group, neighbour(step)), device_id_type=MESH
        )

    far_peers(greet)

    for step in range(-REACH, REACH + 1):
        if step:

            @pl.when(jnp.logical_not(in_range(step)))
            def _(step=step):
                for peer_group in range(groups):
                    window[peer_group * SPAN + step + REACH] = jnp.zeros((8, WIDE), F32)

    for side, step in enumerate((-1, 1)):

        @pl.when(jnp.logical_not(in_range(step)))
        def _(side=side):
            for turn in range(3):
                beside[turn, side] = jnp.zeros((8, WIDE), F32)

    for fetch in fetches[:-2] + fetches[-1:]:
        fetch.wait()
    lane = lax.broadcasted_iota(jnp.int32, (1, 2 * TILE), 1)
    second = lane >= TILE
    slot = jnp.where(second, lane - TILE, lane)
    occ = occ_ref[...]
    live = (slot < jnp.where(second, occ[:, 1:2], occ[:, 0:1])).astype(F32)
    pol = pol_ref[...]
    root = lax.rsqrt(pol)
    pos = pos_ref[...]
    source = dip_ref[...] * live
    place_x = HALF * (pos[0:1] + jnp.where(second, 2.0, 0.0))
    own[0] = jnp.concatenate(
        [place_x, HALF * pos[1:3], root, source, jnp.zeros((1, WIDE), F32)], axis=0
    )
    geo_t[...] = jnp.transpose(own[0])

    series = [jnp.ones_like(pos), pos]
    for _ in range(2, ORDER + 1):
        series.append(2.0 * pos * series[-1] - series[-2])
    cheb = jnp.concatenate(series + [jnp.zeros((5, WIDE), F32)], axis=0)
    planes = dot(pick_ref[...], jnp.concatenate(split(cheb), axis=0), PLAIN)
    mono = planes[0:WIDE] * planes[WIDE : 2 * WIDE] * planes[2 * WIDE :]
    mono_ref[...] = mono
    first_half = jnp.where(second, 0.0, source)
    second_half = source - first_half
    moments = jnp.concatenate([first_half, second_half, jnp.zeros((2, WIDE), F32)], axis=0)
    window[group * SPAN + REACH] = dot_parts(split(moments), split(mono), LANES)

    below = jnp.minimum(layer, REACH)
    above = jnp.minimum(owners - 1 - layer, REACH)
    pl.semaphore_wait(barrier, (below + above + 1) * groups - 1)

    def near_copy(turn, side, step):
        return pltpu.make_async_remote_copy(
            src_ref=own.at[turn],
            dst_ref=beside.at[turn, side],
            send_sem=nsend.at[2 * turn + side],
            recv_sem=nrecv.at[2 * turn + side],
            device_id=(group, neighbour(step)),
            device_id_type=MESH,
        )

    def near_send(turn):
        for side, step in enumerate((1, -1)):
            pl.when(in_range(step))(
                lambda side=side, step=step: near_copy(turn, side, step).start()
            )

    def near_wait(turn):
        for side, step in enumerate((-1, 1)):
            pl.when(in_range(step))(
                lambda side=side, step=step: near_copy(turn, side, step).wait_recv()
            )

    near_send(0)

    def far_send(peer_group, step):
        pltpu.make_async_remote_copy(
            src_ref=window.at[group * SPAN + REACH],
            dst_ref=window.at[group * SPAN + REACH - step],
            send_sem=wsend.at[peer_group * SPAN + REACH + step],
            recv_sem=wrecv.at[group * SPAN + REACH - step],
            device_id=(peer_group, neighbour(step)),
            device_id_type=MESH,
        ).start()

    far_peers(far_send)

    def far_copy(peer_group, step):
        place = peer_group * SPAN + REACH + step
        return pltpu.make_async_remote_copy(
            src_ref=window.at[group * SPAN + REACH],
            dst_ref=window.at[place],
            send_sem=wsend.at[place],
            recv_sem=wrecv.at[place],
            device_id=(peer_group, neighbour(step)),
            device_id_type=MESH,
        )

    def build(layers, size):
        def body(block, carry):
            rows = pl.ds(pl.multiple_of(block * size, size), size)
            target = geo_t[rows, :]
            total = [None] * 3
            for number, load, shift, half in [one + (h,) for one in layers for h in range(2)]:
                geo = load(half)
                delta = [target[:, axis : axis + 1] - geo[axis : axis + 1] for axis in range(2)]
                delta.append(target[:, 2:3] - (geo[2:3] + 2.0 * HALF * shift))
                squared = delta[0] * delta[0] + delta[1] * delta[1] + (delta[2] * delta[2] + SOFT)
                inverse = lax.rsqrt(squared)
                strength = squared * squared * inverse * (THOLE * target[:, 3:4] * geo[3:4])
                damping = jnp.exp(-strength)
                lambda_three = 1.0 - damping
                lambda_five = lambda_three - strength * damping
                inverse_two = inverse * inverse
                cube = inverse_two * inverse
                direct = lambda_three * cube
                radial = 3.0 * lambda_five * (cube * inverse_two)
                if number == 0:
                    shape = (size, TILE)
                    here = block * size + lax.broadcasted_iota(jnp.int32, shape, 0)
                    other = half * TILE + lax.broadcasted_iota(jnp.int32, shape, 1)
                    keep = here != other
                    direct = jnp.where(keep, direct, 0.0)
                    radial = jnp.where(keep, radial, 0.0)
                scaled = [radial * part for part in delta]
                entries = [
                    scaled[0] * delta[0] - direct,
                    scaled[1] * delta[1] - direct,
                    scaled[2] * delta[2] - direct,
                    scaled[0] * delta[1],
                    scaled[0] * delta[2],
                    scaled[1] * delta[2],
                ]
                for index, entry in enumerate(entries):
                    tensor[2 * number + half, index, rows, :] = entry
                total = gather(total, entries, [geo[4:5], geo[5:6], geo[6:7]])
            for axis in range(3):
                if layers[0][0] == 0:
                    acc[axis, rows, :] = total[axis]
                else:
                    acc[axis, rows, :] += total[axis]
            return carry

        lax.fori_loop(0, 2 * TILE // size, body, 0)

    def gather(total, m, q):
        terms = [
            m[0] * q[0] + m[3] * q[1] + m[4] * q[2],
            m[3] * q[0] + m[1] * q[1] + m[5] * q[2],
            m[4] * q[0] + m[5] * q[1] + m[2] * q[2],
        ]
        return [t if old is None else old + t for old, t in zip(total, terms)]

    def apply(numbers, rows_of, first):
        parts = [
            [rows_of(number)[axis : axis + 1, half * TILE : (half + 1) * TILE] for axis in range(3)]
            for number in numbers
            for half in range(2)
        ]

        def body(block, carry):
            rows = pl.ds(pl.multiple_of(block * ROWS, ROWS), ROWS)
            total = [None] * 3 if first else [acc[axis, rows, :] for axis in range(3)]
            for place, number in enumerate(numbers):
                for half in range(2):
                    entries = [tensor[2 * number + half, index, rows, :] for index in range(6)]
                    total = gather(total, entries, parts[2 * place + half])
            for axis in range(3):
                acc[axis, rows, :] = total[axis]
            return carry

        lax.fori_loop(0, 2 * TILE // ROWS, body, 0)

    def collect():
        row = lax.broadcasted_iota(jnp.int32, (8, 2 * TILE), 0)
        total = None
        for axis in range(3):
            unit = (row == axis).astype(F32).astype(BF16)
            part = dot(unit, jnp.concatenate(split(acc[axis]), axis=1), LANES)
            total = part if total is None else total + part
        return total[0:3]

    build([(0, lambda half: own[0, :, half * TILE : (half + 1) * TILE], 0.0)], 32)

    ilist = fbox_ref.shape[1]
    flat_rows = window.shape[0] * 8
    row = lax.broadcasted_iota(jnp.int32, (flat_rows, 1), 0)
    place, inner = row >> 3, row & 7
    owner_group = jnp.zeros_like(place)
    for peer_group in range(1, groups):
        owner_group += (place >= peer_group * SPAN).astype(jnp.int32)
    number = (owner_group * (owners - SPAN) + place + (layer - REACH)) * (FX * FY)
    number = number + (inner >= 3).astype(jnp.int32)
    number = jnp.where(inner < 6, number, -1)
    line = lax.broadcasted_iota(jnp.int32, (64, ilist), 0)
    entry = lax.broadcasted_iota(jnp.int32, (64, ilist), 1)
    selector = None
    for box in range(FX * FY):
        match = (fbox_ref[box : box + 1] == number).astype(F32).astype(BF16)
        inside = line & 7
        mine = jnp.logical_and(inside >= 3 * box, inside < 3 * box + 3)
        mine = jnp.logical_and(mine, entry < fcnt_ref[...][:, box : box + 1])
        mine = jnp.logical_and(mine, fcls_ref[box : box + 1] == (line >> 3))
        weights = split(jnp.where(mine, fscl_ref[box : box + 1], 0.0))
        part = dot(weights[0], match, LANES) + dot(weights[1], match, LANES)
        selector = part if selector is None else selector + part
    left = lax.broadcasted_iota(jnp.int32, selector.shape, 0) & 7
    right = lax.broadcasted_iota(jnp.int32, selector.shape, 1) & 7
    left = jnp.where(left >= 3, left - 3, left)
    right = jnp.where(right >= 3, right - 3, right)
    selector = split(jnp.where(left == right, selector, 0.0))

    near_wait(0)
    build(
        [
            (side + 1, lambda half, side=side: beside[0, side, :, half * TILE : (half + 1) * TILE], shift)
            for side, shift in enumerate((-1.0, 1.0))
        ],
        16,
    )
    near_zero = collect()

    fetches[-2].wait()
    nterm, classes = trans_ref.shape[:2]
    shifted = split(trans_ref[...].reshape(nterm * classes, nterm))
    fold_shape = (nterm * classes, nterm)
    fold = lax.broadcasted_iota(jnp.int32, fold_shape, 0) >> 3
    fold = (fold == lax.broadcasted_iota(jnp.int32, fold_shape, 1)).astype(F32).astype(BF16)
    far_peers(lambda peer_group, step: far_copy(peer_group, step).wait_recv())
    summed = dot_parts(selector, split(window[...].reshape(flat_rows, WIDE)), PLAIN)
    moved = dot_parts(split(summed[:, 0:nterm]), shifted, LANES)
    wanted = lax.broadcasted_iota(jnp.int32, (8, nterm * classes), 1) & 7
    merged = None
    for index in range(classes):
        part = jnp.where(wanted == index, moved[8 * index : 8 * index + 8], 0.0)
        merged = part if merged is None else merged + part
    merged = split(merged)
    local = dot(merged[0], fold, PLAIN) + dot(merged[1], fold, PLAIN)
    spread = dot_parts(split(local), split(mono_ref[0:nterm]), PLAIN)
    far_part = jnp.where(second, spread[3:6], spread[0:3])

    residual = live * (perm_ref[...] + far_part + near_zero - source / pol)
    res_ref[...] = residual
    sweep = pol * residual
    for turn in (1, 2):
        own[turn] = jnp.concatenate([sweep, jnp.zeros((5, WIDE), F32)], axis=0)
        near_send(turn)
        apply((0,), lambda _, turn=turn: own[turn], True)
        near_wait(turn)
        apply((1, 2), lambda number, turn=turn: beside[turn, number - 1], False)
        sweep = live * pol * (residual + collect())
    new_ref[...] = source + sweep

    for turn in range(3):
        for side, step in enumerate((1, -1)):
            pl.when(in_range(step))(
                lambda turn=turn, side=side, step=step: near_copy(turn, side, step).wait_send()
            )
    far_peers(lambda peer_group, step: far_copy(peer_group, step).wait_send())


def staged(groups, owners, *refs):
    given, results, held, rest, arrived = refs[:11], refs[11:13], refs[13:24], refs[24:-1], refs[-1]
    fetches = [
        pltpu.make_async_copy(given[index], held[index], arrived.at[index]) for index in range(11)
    ]
    for fetch in fetches:
        fetch.start()
    kernel(groups, owners, *held, *results, *rest, fetches)


def solution(mesh):
    groups, owners = mesh.shape["group"], mesh.shape["box"]

    def on_device(dip, perm, pos, pol, occ, fbox, fcls, fcnt, fscl, trans):
        vmem = pl.BlockSpec(memory_space=pltpu.VMEM)
        slots = groups * SPAN
        operands = (
            dip, perm, pos, pol.reshape(1, -1), occ.reshape(1, -1), fbox, fcls,
            fcnt.reshape(1, -1), fscl, jnp.transpose(trans, (1, 0, 2)),
            jnp.asarray(pick_matrix(), BF16),
        )
        return pl.pallas_call(
            functools.partial(staged, groups, owners),
            out_shape=(jax.ShapeDtypeStruct(dip.shape, F32),) * 2,
            in_specs=[pl.BlockSpec(memory_space=pltpu.HBM)] * 11,
            out_specs=(vmem, vmem),
            scratch_shapes=[pltpu.VMEM(one.shape, one.dtype) for one in operands]
            + [
                pltpu.VMEM((3, 8, WIDE), F32),
                pltpu.VMEM((3, 2, 8, WIDE), F32),
                pltpu.VMEM((WIDE, 8), F32),
                pltpu.VMEM((WIDE, WIDE), F32),
                pltpu.VMEM((slots, 8, WIDE), F32),
                pltpu.VMEM((6, 6, 2 * TILE, TILE), F32),
                pltpu.VMEM((3, 2 * TILE, TILE), F32),
                pltpu.SemaphoreType.DMA((6,)),
                pltpu.SemaphoreType.DMA((6,)),
                pltpu.SemaphoreType.DMA((slots,)),
                pltpu.SemaphoreType.DMA((slots,)),
                pltpu.SemaphoreType.DMA((11,)),
            ],
            compiler_params=pltpu.CompilerParams(
                collective_id=0, has_side_effects=True, vmem_limit_bytes=64 * 1024 * 1024
            ),
        )(*operands)

    split_dim = ("group", "box")
    return jax.shard_map(
        on_device,
        mesh=mesh,
        in_specs=(
            P(None, split_dim), P(None, split_dim), P(None, split_dim), P(split_dim),
            P(split_dim), P(split_dim, None), P(split_dim, None), P(split_dim),
            P(split_dim, None), P(),
        ),
        out_specs=(P(None, split_dim), P(None, split_dim)),
        check_vma=False,
    )
```
